32 devices in a mesh: dp: 2 (over y), label: 8 (over z, x), tensor: 2 (over core).
Axes of the slice: x: 2, y: 2, z: 4, core: 2. Of those that a mesh axis runs over, the one named last changes fastest.
Arguments:
- hidden: bfloat16 [2048, 3584], P('dp', 'label'), may hold values from -6 to 6
- enc_weight: bfloat16 [3584, 3584], P('label', 'tensor'), may hold values from -0.09375 to 0.09375
- enc_gain: float32 [3584], P('tensor'), may hold values from 0.25 to 1.75
- head_weight: bfloat16 [16, 256, 3584], P('label', None, 'tensor'), may hold values from -0.09375 to 0.09375
- propensity: float32 [16, 256], P('label'), may hold values from 0.25 to 1
- blocks: int32 [2048, 8], P(('dp', 'label')), may hold values from 0 to 15, all different within a row; in each aligned block of 128 rows (0 to 127, 128 to 255, ...) at most 128 rows name the same one
- offsets: int32 [2048, 2], P(('dp', 'label')), may hold values from 0 to 255
Outputs:
- enc_grad: float32 [3584, 3584], P('label', 'tensor')
- head_grad: float32 [16, 256, 3584], P('label', 'dp', 'tensor')
The draws below stay inside these ranges and needn't reach their ends.
Inputs may be any that keep to these rules, and one draw needn't show every extreme that they name: Each row names 8 different blocks. Among the rows of one device no block is named more than 128 times, and in every draw some block is named exactly 128 times by the rows of some device.
All inputs are finite; a program needn't handle non-finite values.
Results may differ from the reference program's by a relative error of at most 0.014.
Values may be sent and summed in bfloat16 or wider, within the bound.
A program may use at most 128 MiB of HBM per device.

```python
import math
import jax
import jax.numpy as jnp
import numpy as np
from jax import lax

D = 3584
BLK = 256
POS = 2
K = 8
ROWS_DEV = 128
NBLK = 16
MOST = 128
ROWS = 2048
N_LABEL = 8


def set_ends(result, own_key, smallest, high):
    longest = result.shape.index(max(result.shape))
    spots = []
    for shift in (0, 1):
        where = [jax.random.randint(jax.random.fold_in(own_key, axis), (), 0, length) for axis, length in enumerate(result.shape)]
        where[longest] = (where[longest] + shift) % result.shape[longest]
        spots.append(tuple(where))
    return result.at[spots[0]].set(smallest).at[spots[1]].set(high)


def steps_of(own_key, extent, pieces, least, top_value):
    def one(dim, shards_of):
        draws = jax.random.uniform(jax.random.fold_in(jax.random.fold_in(own_key, 6), dim), (shards_of,), jnp.float32, least / len(pieces), top_value / len(pieces))
        return jnp.repeat(jnp.exp(draws), extent[dim] // shards_of).reshape((-1,) + (1,) * (len(extent) - dim - 1))

    level = one(*pieces[0])
    for cut in pieces[1:]:
        level = level * one(*cut)
    return level


def shared_out(stream_key, own, number, rows, number_of, top, limit, slope):
    order = jax.random.permutation(stream_key, number_of)
    crowded, common = shares(number_of, rows * top, limit, slope, True), shares(number_of, rows * top, limit, slope, False)
    places = jnp.arange(number_of)

    def named(lengths, rotation):
        used = int((lengths > 0).sum())
        fixed = max(1, used // 4)
        moved = fixed + (places - fixed + rotation * (used - fixed)) % max(1, number_of - fixed)
        return jnp.zeros((number_of,), jnp.int32).at[order[jnp.where(places < fixed, places, moved)]].set(jnp.asarray(lengths, jnp.int32))

    lengths = jnp.where(number % 4 == 0, named(crowded, number // 4), named(common, number - number // 4 - 1))
    mixed = jax.random.permutation(jax.random.fold_in(own, 3), number_of)
    donor, taker = mixed[0:number_of // 2 * 2:2], mixed[1:number_of // 2 * 2:2]
    margin = jnp.minimum(lengths[donor] - 1, limit - lengths[taker]) // 2
    margin = jnp.where((donor == order[0]) | (taker == order[0]) | (lengths[taker] == 0), 0, jnp.maximum(margin, 0))
    moved = jax.random.randint(jax.random.fold_in(own, 4), (number_of // 2,), 0, 1 << 20) % (margin + 1)
    lengths = lengths.at[donor].add(-moved).at[taker].add(moved)
    labels = jnp.searchsorted(jnp.cumsum(lengths), jnp.arange(rows * top), side="right").astype(jnp.int32)
    listing = labels.reshape(top, rows).T
    listing = listing[jax.random.permutation(jax.random.fold_in(own, 1), rows)]
    rotation = jax.random.randint(jax.random.fold_in(own, 2), (rows, 1), 0, top)
    return jnp.take_along_axis(listing, (jnp.arange(top)[None, :] + rotation) % top, axis=1)


def shares(number_of, total, limit, slope, full):
    weights = [(1 << 20) // math.isqrt(standing ** slope) + 1 for standing in range(1, number_of + 1)]
    largest = limit if full else min(limit, max(-(-total // number_of), total * weights[0] // sum(weights)))
    least = 1 if total - largest >= number_of - 1 else 0
    counts, surplus = [largest] + [least] * (number_of - 1), total - largest - least * (number_of - 1)
    while surplus > 0:
        free = [i for i in range(1, number_of) if counts[i] < largest] or [i for i in range(1, number_of) if counts[i] < limit]
        whole, budget = sum([weights[i] for i in free]), surplus
        for i in free:
            more = min(limit - counts[i], max(1, budget * weights[i] // whole), surplus)
            counts[i] = counts[i] + more
            surplus = surplus - more
    return np.array(counts)


def centred(own_key, shape, scale, reach, split=(), kind=jnp.bfloat16):
    drawn = jax.random.normal(own_key, shape, jnp.float32) * scale
    if len(split) > 0:
        drawn = steps_of(own_key, shape, split, -0.22, 0.18) * drawn
    return jnp.clip(drawn, min=-reach, max=reach).astype(kind)


def setup_inputs(seed: int = 0) -> dict:
    seeds = jax.random.split(jax.random.key(seed), 8)
    hidden = centred(seeds[0], (ROWS, D), 1.0, 6.0, ((0, 2), (1, 8)))
    enc_weight = centred(seeds[1], (D, D), D ** -0.5, 0.09375, ((0, 8), (1, 2)))
    enc_gain = jnp.clip(1.0 + 0.15 * jax.random.normal(seeds[2], (D,), jnp.float32), 0.25, 1.75)
    head_weight = centred(seeds[3], (NBLK, BLK, D), D ** -0.5, 0.09375, ((0, 8), (2, 2)))
    propensity = jnp.clip(jnp.exp(math.log(1.0) - 1.3862944 * jax.random.uniform(seeds[4], (NBLK, BLK), jnp.float32) ** steps_of(seeds[4], (NBLK, BLK), ((0, 8),), -0.2, 0.2)), 0.25, 1.0)
    blocks_keys = jax.random.split(jax.random.fold_in(seeds[5], 1), ROWS // ROWS_DEV)
    blocks_turns = jax.random.permutation(jax.random.fold_in(seeds[5], 3), ROWS // ROWS_DEV)
    blocks = jax.vmap(lambda own, number: shared_out(jax.random.fold_in(seeds[5], 2), own, number, ROWS_DEV, NBLK, K, MOST, 2))(blocks_keys, blocks_turns).reshape((ROWS, K))
    offsets = set_ends(jax.random.randint(seeds[6], (ROWS, POS), 0, BLK), jax.random.fold_in(seeds[6], 1), 0, BLK - 1).astype(jnp.int32)
    return dict(hidden=hidden, enc_weight=enc_weight, enc_gain=enc_gain, head_weight=head_weight, propensity=propensity, blocks=blocks, offsets=offsets)


EPSILON = 1e-06

def reference(hidden, enc_weight, enc_gain, head_weight, propensity, blocks, offsets):
    group_width = D // N_LABEL

    def add_group(index, running):
        first_col = (index * group_width).astype(jnp.int32)
        columns = lax.dynamic_slice_in_dim(hidden, first_col, group_width, 1)
        weight_rows = lax.dynamic_slice_in_dim(enc_weight, first_col, group_width, 0)
        product = jnp.dot(columns, weight_rows, preferred_element_type=jnp.float32)
        rounded = lax.optimization_barrier(product.astype(jnp.bfloat16))
        return running + rounded.astype(jnp.float32)
    pooled = lax.fori_loop(0, N_LABEL, add_group, jnp.zeros((ROWS, D), jnp.float32))
    inverse = lax.rsqrt(lax.optimization_barrier(jnp.mean(pooled * pooled, axis=1)) + EPSILON)
    embedded = (pooled * inverse[:, None] * enc_gain[None, :]).astype(jnp.bfloat16)
    label_ids = jnp.arange(BLK, dtype=jnp.int32)
    slot_ids = jnp.arange(K, dtype=jnp.int32)

    def per_block(embed_grad, block_id):
        matched = blocks == block_id
        present = jnp.any(matched, axis=1)
        slot_of = lax.optimization_barrier(jnp.sum(jnp.where(matched, slot_ids[None, :], 0), axis=1)).astype(jnp.int32)
        pos_slot = present & (slot_of < POS)
        picked = jnp.take_along_axis(offsets, jnp.minimum(slot_of, POS - 1)[:, None], axis=1)[:, 0]
        vectors = head_weight[block_id]
        scores = jnp.dot(embedded, vectors.T, preferred_element_type=jnp.float32)
        positive = pos_slot[:, None] & (picked[:, None] == label_ids[None, :])
        weight_pos = (1.0 / propensity[block_id])[None, :]
        above = jnp.maximum(1.0 - scores, 0.0)
        below = jnp.maximum(1.0 + scores, 0.0)
        slopes = jnp.where(positive, -2.0 * weight_pos * above + 2.0 * (1.0 - weight_pos) * below, 2.0 * below)
        slopes = jnp.where(present[:, None], slopes / ROWS_DEV, 0.0).astype(jnp.bfloat16)
        back_terms = jnp.dot(slopes, vectors, preferred_element_type=jnp.float32)
        back_terms = lax.optimization_barrier(back_terms.astype(jnp.bfloat16)).astype(jnp.float32)
        block_grad = lax.dot_general(slopes, embedded, (((0,), (0,)), ((), ())), preferred_element_type=jnp.float32)
        return (embed_grad + back_terms, block_grad)
    embed_grad, head_grad = lax.scan(per_block, jnp.zeros((ROWS, D), jnp.float32), jnp.arange(NBLK, dtype=jnp.int32))
    scaled = embed_grad * enc_gain[None, :]
    row_dot = lax.optimization_barrier(jnp.sum(scaled * pooled, axis=1))
    pooled_grad = (inverse[:, None] * (scaled - pooled * (inverse * inverse * row_dot / D)[:, None])).astype(jnp.bfloat16)
    enc_grad = lax.dot_general(hidden, pooled_grad, (((0,), (0,)), ((), ())), preferred_element_type=jnp.float32)
    return (enc_grad, head_grad)
```

```python
import jax
import jax.numpy as jnp
from jax import lax
from jax.sharding import PartitionSpec as P

EPSILON = 1e-06
F32 = jnp.float32
BF16 = jnp.bfloat16


def sum_over_dp(part):
    n = lax.axis_size("dp")
    if n == 2:
        other = lax.ppermute(part.astype(BF16), "dp", [(0, 1), (1, 0)])
        return part + other.astype(F32)
    return lax.psum(part.astype(BF16), "dp").astype(F32)


def scatter_over_dp(part):
    n = lax.axis_size("dp")
    if n == 2:
        half = part.shape[1] // 2
        me = lax.axis_index("dp")
        mine = lax.dynamic_slice_in_dim(part, me * half, half, 1)
        theirs = lax.dynamic_slice_in_dim(part, (1 - me) * half, half, 1)
        other = lax.ppermute(theirs.astype(BF16), "dp", [(0, 1), (1, 0)])
        return mine + other.astype(F32)
    return lax.psum_scatter(part.astype(BF16), "dp", scatter_dimension=1, tiled=True).astype(F32)


def shards(hidden, enc_weight, enc_gain, head_weight, propensity, blocks, offsets):
    width_half = enc_weight.shape[1]
    rows_here = blocks.shape[0]
    pos_count = offsets.shape[1]
    blocks_dev, block_size = head_weight.shape[:2]
    full_width = width_half * lax.axis_size("tensor")
    head = head_weight.reshape(blocks_dev * block_size, width_half)

    all_blocks = lax.all_gather(
        jnp.concatenate([blocks, offsets], axis=1), "label", axis=0, tiled=True
    )
    all_offsets = all_blocks[:, blocks.shape[1] :]
    all_blocks = all_blocks[:, : blocks.shape[1]]

    product = jnp.dot(hidden, enc_weight, preferred_element_type=F32).astype(BF16)
    pooled = lax.psum_scatter(product, "label", scatter_dimension=0, tiled=True).astype(F32)
    squares = lax.psum(jnp.sum(pooled * pooled, axis=1), "tensor")
    inverse = lax.rsqrt(squares / full_width + EPSILON)
    embedded = (pooled * inverse[:, None] * enc_gain[None, :]).astype(BF16)
    rows = lax.all_gather(embedded, "label", axis=0, tiled=True)

    partial = lax.dot_general(
        rows, head, (((1,), (1,)), ((), ())), preferred_element_type=F32
    )
    scores = lax.psum(partial.astype(BF16), "tensor").astype(F32)

    label_ids = jnp.arange(block_size, dtype=jnp.int32)[None, :]
    first = lax.axis_index("label") * blocks_dev
    pieces = []
    for n in range(blocks_dev):
        named = all_blocks == first + n
        present = jnp.any(named, axis=1)[:, None]
        positive = jnp.zeros((), bool)
        for k in range(pos_count):
            positive = positive | (
                named[:, k : k + 1] & (all_offsets[:, k : k + 1] == label_ids)
            )
        here = scores[:, n * block_size : (n + 1) * block_size]
        weight_pos = (1.0 / propensity[n])[None, :]
        above = jnp.maximum(1.0 - here, 0.0)
        below = jnp.maximum(1.0 + here, 0.0)
        slope = jnp.where(
            positive, -2.0 * weight_pos * above + 2.0 * (1.0 - weight_pos) * below, 2.0 * below
        )
        pieces.append(jnp.where(present, slope / rows_here, 0.0).astype(BF16))
    slopes = jnp.concatenate(pieces, axis=1)

    back = jnp.dot(slopes, head, preferred_element_type=F32).astype(BF16)
    embed_grad = lax.psum_scatter(back, "label", scatter_dimension=0, tiled=True).astype(F32)

    head_partial = lax.dot_general(
        slopes, rows, (((0,), (0,)), ((), ())), preferred_element_type=F32
    ).reshape(blocks_dev, block_size, width_half)
    head_grad = scatter_over_dp(head_partial)

    scaled = embed_grad * enc_gain[None, :]
    row_dot = lax.psum(jnp.sum(scaled * pooled, axis=1), "tensor")
    pooled_grad = (
        inverse[:, None] * (scaled - pooled * (inverse * inverse * row_dot / full_width)[:, None])
    ).astype(BF16)
    all_grad = lax.all_gather(pooled_grad, "label", axis=0, tiled=True)
    weight_part = lax.dot_general(
        hidden, all_grad, (((0,), (0,)), ((), ())), preferred_element_type=F32
    )
    enc_grad = sum_over_dp(weight_part)
    return (enc_grad, head_grad)


def solution(mesh):
    in_specs = (
        P("dp", "label"),
        P("label", "tensor"),
        P("tensor"),
        P("label", None, "tensor"),
        P("label", None),
        P(("dp", "label"), None),
        P(("dp", "label"), None),
    )
    out_specs = (P("label", "tensor"), P("label", "dp", "tensor"))
    return jax.shard_map(shards, mesh=mesh, in_specs=in_specs, out_specs=out_specs, check_vma=False)
```

```python
import functools

import jax
import jax.numpy as jnp
from jax import lax
from jax.experimental import pallas as pl
from jax.experimental.pallas import tpu as pltpu
from jax.sharding import PartitionSpec as P

EPSILON = 1e-06
F32 = jnp.float32
BF16 = jnp.bfloat16


MESH = pl.DeviceIdType.MESH
FAST = 2
VMEM_LIMIT = 40 * 1024 * 1024


def spot():
    me = lax.axis_index("label")
    return me // FAST, lax.rem(me, FAST)


def at(axis, index):
    here = {name: lax.axis_index(name) for name in ("dp", "label", "tensor")}
    here[axis] = index
    return (here["dp"], here["label"], here["tensor"])


def greet(devices):
    barrier = pltpu.get_barrier_semaphore()
    for device in devices:
        pl.semaphore_signal(barrier, inc=1, device_id=device, device_id_type=MESH)
    pl.semaphore_wait(barrier, len(devices))


def neighbours(high, low, z, length):
    found = [at("label", z * FAST + 1 - low)]
    if z + 1 < length:
        found.append(at("label", (z + 1) * FAST + low))
    if z > 0:
        found.append(at("label", (z - 1) * FAST + low))
    return found


def gather_kernel(length, count, *refs):
    sources, gathered = refs[:count], refs[count : 2 * count]
    send_sem, recv_sem = refs[2 * count :]
    high, low = spot()

    def copies(way, block, first, device):
        return [
            pltpu.make_async_remote_copy(
                src_ref=sources[i] if first else gathered[i].at[block],
                dst_ref=gathered[i].at[block],
                send_sem=send_sem.at[i, way, block],
                recv_sem=recv_sem.at[i, block],
                device_id=device,
                device_id_type=MESH,
            )
            for i in range(count)
        ]

    def branch(z):
        across = at("label", z * FAST + 1 - low)
        up = at("label", (z + 1) * FAST + low)
        down = at("label", (z - 1) * FAST + low)
        greet(neighbours(high, low, z, length))
        sent = []

        def send(way, block, first, device):
            made = copies(way, block, first, device)
            for copy in made:
                copy.start()
            sent.extend(made)

        def arrived(block):
            for copy in copies(0, block, False, across):
                copy.wait_recv()

        own = z * FAST + low
        if z + 1 < length:
            send(1, own, True, up)
        if z > 0:
            send(2, own, True, down)
        send(0, own, True, across)
        for i in range(count):
            gathered[i][own] = sources[i][...]
        for step in range(1, length):
            if z - step >= 0:
                block = (z - step) * FAST + low
                arrived(block)
                if z + 1 < length:
                    send(1, block, False, up)
                send(0, block, False, across)
            if z + step < length:
                block = (z + step) * FAST + low
                arrived(block)
                if z > 0:
                    send(2, block, False, down)
                send(0, block, False, across)
        for other in sorted(range(length), key=lambda t: abs(t - z)):
            arrived(other * FAST + 1 - low)
        for copy in sent:
            copy.wait_send()

    for z in range(length):
        pl.when(high == z)(functools.partial(branch, z))


def gather_label(arrays, number):
    devices = lax.axis_size("label")
    if devices != 4 * FAST:
        return [lax.all_gather(a, "label", axis=0) for a in arrays]
    count = len(arrays)
    return pl.pallas_call(
        functools.partial(gather_kernel, devices // FAST, count),
        out_shape=[jax.ShapeDtypeStruct((devices,) + a.shape, a.dtype) for a in arrays],
        in_specs=[pl.BlockSpec(memory_space=pltpu.VMEM)] * count,
        out_specs=[pl.BlockSpec(memory_space=pltpu.VMEM)] * count,
        scratch_shapes=[
            pltpu.SemaphoreType.DMA((count, 3, devices)),
            pltpu.SemaphoreType.DMA((count, devices)),
        ],
        compiler_params=pltpu.CompilerParams(
            collective_id=number, has_side_effects=True, vmem_limit_bytes=VMEM_LIMIT
        ),
    )(*arrays)


def scatter_kernel(length, swap, *refs):
    if swap:
        parts, theirs, out, other = refs[:4]
        rest = refs[4:]
    else:
        parts, out = refs[:2]
        rest = refs[2:]
    crossed, in_up, in_down, out_up, out_down, send_sem, recv_sem, swap_sem = rest
    high, low = spot()
    rows = parts.shape[1]
    tile = 16

    def remote(src, dst, way, t, device):
        return pltpu.make_async_remote_copy(
            src_ref=src,
            dst_ref=dst,
            send_sem=send_sem.at[way, t],
            recv_sem=recv_sem.at[way, t],
            device_id=device,
            device_id_type=MESH,
        )

    def branch(z):
        across = at("label", z * FAST + 1 - low)
        up = at("label", (z + 1) * FAST + low)
        down = at("label", (z - 1) * FAST + low)
        greeted = neighbours(high, low, z, length)
        if swap:
            beside = at("dp", 1 - lax.axis_index("dp"))
            greeted.append(beside)
        greet(greeted)
        sent = []
        if swap:
            exchange = pltpu.make_async_remote_copy(
                src_ref=theirs,
                dst_ref=other,
                send_sem=swap_sem.at[0],
                recv_sem=swap_sem.at[1],
                device_id=beside,
                device_id_type=MESH,
            )
            exchange.start()

        order = sorted(range(length), key=lambda t: (-abs(t - z), -t))

        def cross(t):
            copy = remote(parts.at[t * FAST + 1 - low], crossed.at[t], 0, t, across)
            copy.start()
            sent.append(copy)

        def total(t, terms, result):
            def body(i, carry):
                span = pl.ds(pl.multiple_of(i * tile, tile), tile)
                value = parts[t * FAST + low, span].astype(F32) + crossed[t, span].astype(F32)
                for term in terms:
                    value += term[t, span].astype(F32)
                if result is None:
                    out[span] = value
                else:
                    result[t, span] = value.astype(BF16)
                return carry

            lax.fori_loop(0, rows // tile, body, 0)

        for t in order[:2]:
            cross(t)
        for place, t in enumerate(order):
            remote(parts.at[0], crossed.at[t], 0, t, across).wait_recv()
            if place + 2 < length:
                cross(order[place + 2])
            terms = []
            if t >= z and z > 0:
                remote(out_up.at[t], in_up.at[t], 1, t, across).wait_recv()
                terms.append(in_up)
            if t <= z and z + 1 < length:
                remote(out_down.at[t], in_down.at[t], 2, t, across).wait_recv()
                terms.append(in_down)
            if t > z:
                total(t, terms, out_up)
                copy = remote(out_up.at[t], in_up.at[t], 1, t, up)
            elif t < z:
                total(t, terms, out_down)
                copy = remote(out_down.at[t], in_down.at[t], 2, t, down)
            else:
                total(t, terms, None)
                continue
            copy.start()
            sent.append(copy)
        for copy in sent:
            copy.wait_send()
        if swap:
            exchange.wait()

    for z in range(length):
        pl.when(high == z)(functools.partial(branch, z))


def scatter_label(parts, number, theirs=None):
    devices, rows, width = parts.shape
    swap = theirs is not None
    if devices != 4 * FAST:
        out = lax.psum_scatter(parts, "label", scatter_dimension=0, tiled=False).astype(F32)
        if swap:
            return out, lax.ppermute(theirs, "dp", [(0, 1), (1, 0)])
        return out
    length = devices // FAST
    out_shape = [jax.ShapeDtypeStruct((rows, width), F32)]
    operands = [parts]
    if swap:
        out_shape.append(jax.ShapeDtypeStruct(theirs.shape, theirs.dtype))
        operands.append(theirs)
    outs = pl.pallas_call(
        functools.partial(scatter_kernel, length, swap),
        out_shape=out_shape,
        in_specs=[pl.BlockSpec(memory_space=pltpu.VMEM)] * len(operands),
        out_specs=[pl.BlockSpec(memory_space=pltpu.VMEM)] * len(operands),
        scratch_shapes=[pltpu.VMEM((length, rows, width), BF16)] * 5
        + [
            pltpu.SemaphoreType.DMA((3, length)),
            pltpu.SemaphoreType.DMA((3, length)),
            pltpu.SemaphoreType.DMA((2,)),
        ],
        compiler_params=pltpu.CompilerParams(
            collective_id=number, has_side_effects=True, vmem_limit_bytes=VMEM_LIMIT
        ),
    )(*operands)
    return outs if swap else outs[0]


def sum_over_dp(part):
    n = lax.axis_size("dp")
    if n == 2:
        other = lax.ppermute(part.astype(BF16), "dp", [(0, 1), (1, 0)])
        return part + other.astype(F32)
    return lax.psum(part.astype(BF16), "dp").astype(F32)


def shards(hidden, enc_weight, enc_gain, head_weight, propensity, blocks, offsets):
    width_half = enc_weight.shape[1]
    rows_here = blocks.shape[0]
    pos_count = offsets.shape[1]
    blocks_dev, block_size = head_weight.shape[:2]
    full_width = width_half * lax.axis_size("tensor")
    head = head_weight.reshape(blocks_dev * block_size, width_half)

    labels_n = lax.axis_size("label")
    slots = blocks.shape[1]
    targets = jnp.concatenate([blocks, offsets], axis=1).T
    targets = jnp.pad(targets, ((0, -targets.shape[0] % 8), (0, 0)))

    product = jnp.dot(hidden, enc_weight, preferred_element_type=F32).astype(BF16)
    pooled = scatter_label(product.reshape(labels_n, rows_here, width_half), 0)
    squares = lax.psum(jnp.sum(pooled * pooled, axis=1), "tensor")
    inverse = lax.rsqrt(squares / full_width + EPSILON)
    embedded = (pooled * inverse[:, None] * enc_gain[None, :]).astype(BF16)
    rows, targets = gather_label([embedded, targets], 1)
    rows = rows.reshape(labels_n * rows_here, width_half)
    targets = jnp.swapaxes(targets, 1, 2).reshape(labels_n * rows_here, -1)
    all_blocks, all_offsets = targets[:, :slots], targets[:, slots : slots + pos_count]

    partial = lax.dot_general(
        rows, head, (((1,), (1,)), ((), ())), preferred_element_type=F32
    )
    scores = lax.psum(partial.astype(BF16), "tensor").astype(F32)

    label_ids = jnp.arange(block_size, dtype=jnp.int32)[None, :]
    first = lax.axis_index("label") * blocks_dev
    pieces = []
    for n in range(blocks_dev):
        named = all_blocks == first + n
        present = jnp.any(named, axis=1)[:, None]
        positive = jnp.zeros((), bool)
        for k in range(pos_count):
            positive = positive | (
                named[:, k : k + 1] & (all_offsets[:, k : k + 1] == label_ids)
            )
        here = scores[:, n * block_size : (n + 1) * block_size]
        weight_pos = (1.0 / propensity[n])[None, :]
        above = jnp.maximum(1.0 - here, 0.0)
        below = jnp.maximum(1.0 + here, 0.0)
        slope = jnp.where(
            positive, -2.0 * weight_pos * above + 2.0 * (1.0 - weight_pos) * below, 2.0 * below
        )
        pieces.append(jnp.where(present, slope / rows_here, 0.0).astype(BF16))
    slopes = jnp.concatenate(pieces, axis=1)

    back = jnp.dot(slopes, head, preferred_element_type=F32).astype(BF16)
    back = back.reshape(labels_n, rows_here, width_half)
    head_partial = lax.dot_general(
        slopes, rows, (((0,), (0,)), ((), ())), preferred_element_type=F32
    ).reshape(blocks_dev, block_size, width_half)
    if lax.axis_size("dp") == 2:
        half = block_size // 2
        me = lax.axis_index("dp")
        mine = lax.dynamic_slice_in_dim(head_partial, me * half, half, 1)
        theirs = lax.dynamic_slice_in_dim(head_partial, (1 - me) * half, half, 1)
        embed_grad, other = scatter_label(back, 2, theirs.astype(BF16))
        head_grad = mine + other.astype(F32)
    else:
        embed_grad = scatter_label(back, 2)
        head_grad = lax.psum_scatter(
            head_partial.astype(BF16), "dp", scatter_dimension=1, tiled=True
        ).astype(F32)

    scaled = embed_grad * enc_gain[None, :]
    row_dot = lax.psum(jnp.sum(scaled * pooled, axis=1), "tensor")
    pooled_grad = (
        inverse[:, None] * (scaled - pooled * (inverse * inverse * row_dot / full_width)[:, None])
    ).astype(BF16)
    (all_grad,) = gather_label([pooled_grad], 3)
    all_grad = all_grad.reshape(labels_n * rows_here, width_half)
    weight_part = lax.dot_general(
        hidden, all_grad, (((0,), (0,)), ((), ())), preferred_element_type=F32
    )
    enc_grad = sum_over_dp(weight_part)
    return (enc_grad, head_grad)


def solution(mesh):
    in_specs = (
        P("dp", "label"),
        P("label", "tensor"),
        P("tensor"),
        P("label", None, "tensor"),
        P("label", None),
        P(("dp", "label"), None),
        P(("dp", "label"), None),
    )
    out_specs = (P("label", "tensor"), P("label", "dp", "tensor"))
    return jax.shard_map(shards, mesh=mesh, in_specs=in_specs, out_specs=out_specs, check_vma=False)
```

```python
import functools

import jax
import jax.numpy as jnp
from jax import lax
from jax.experimental import pallas as pl
from jax.experimental.pallas import tpu as pltpu
from jax.sharding import PartitionSpec as P

EPSILON = 1e-06
F32 = jnp.float32
BF16 = jnp.bfloat16


MESH = pl.DeviceIdType.MESH
FAST = 2
VMEM_LIMIT = 40 * 1024 * 1024


def spot():
    me = lax.axis_index("label")
    return me // FAST, lax.rem(me, FAST)


def at(axis, index):
    here = {name: lax.axis_index(name) for name in ("dp", "label", "tensor")}
    here[axis] = index
    return (here["dp"], here["label"], here["tensor"])


def greet(devices):
    barrier = pltpu.get_barrier_semaphore()
    for device in devices:
        pl.semaphore_signal(barrier, inc=1, device_id=device, device_id_type=MESH)
    pl.semaphore_wait(barrier, len(devices))


def neighbours(high, low, z, length):
    found = [at("label", z * FAST + 1 - low)]
    if z + 1 < length:
        found.append(at("label", (z + 1) * FAST + low))
    if z > 0:
        found.append(at("label", (z - 1) * FAST + low))
    return found


def hop_copy(held, block, cols, way, part, sems, device):
    send_sem, recv_sem = sems
    return pltpu.make_async_remote_copy(
        src_ref=held.at[block, :, cols],
        dst_ref=held.at[block, :, cols],
        send_sem=send_sem.at[part, way, block],
        recv_sem=recv_sem.at[part, block],
        device_id=device,
        device_id_type=MESH,
    )


def devices_of(z, low):
    return (
        at("label", z * FAST + 1 - low),
        at("label", (z + 1) * FAST + low),
        at("label", (z - 1) * FAST + low),
    )


def send_own(z, low, length, held, cols, part, sems):
    own = z * FAST + low
    across, up, down = devices_of(z, low)
    if z + 1 < length:
        hop_copy(held, own, cols, 1, part, sems, up).start()
    if z > 0:
        hop_copy(held, own, cols, 2, part, sems, down).start()
    hop_copy(held, own, cols, 0, part, sems, across).start()


def forward(z, low, length, held, cols, part, sems):
    across, up, down = devices_of(z, low)
    for step in range(1, length):
        if z - step >= 0:
            block = (z - step) * FAST + low
            hop_copy(held, block, cols, 0, part, sems, across).wait_recv()
            if z + 1 < length:
                hop_copy(held, block, cols, 1, part, sems, up).start()
            hop_copy(held, block, cols, 0, part, sems, across).start()
        if z + step < length:
            block = (z + step) * FAST + low
            hop_copy(held, block, cols, 0, part, sems, across).wait_recv()
            if z > 0:
                hop_copy(held, block, cols, 2, part, sems, down).start()
            hop_copy(held, block, cols, 0, part, sems, across).start()


def wait_sent(z, low, length, held, cols, part, sems):
    across, up, down = devices_of(z, low)
    for t in range(length):
        block = t * FAST + low
        hop_copy(held, block, cols, 0, part, sems, across).wait_send()
        if t <= z and z + 1 < length:
            hop_copy(held, block, cols, 1, part, sems, up).wait_send()
        if t >= z and z > 0:
            hop_copy(held, block, cols, 2, part, sems, down).wait_send()


def by_place(length, high, body):
    for z in range(length):
        pl.when(high == z)(functools.partial(body, z))


def score_kernel(length, rows_ref, target_ref, head_ref, held, targets, scores, *rest):
    leaving, coming, send_sem, recv_sem, pair_send, pair_recv = rest
    high, low = spot()
    own = high * FAST + low
    every = slice(None)
    sems = (send_sem, recv_sem)
    sibling = at("tensor", 1 - lax.axis_index("tensor"))
    held[own] = rows_ref[...]
    targets[own] = target_ref[...]

    def start(z):
        greet(neighbours(high, low, z, length) + [sibling])
        send_own(z, low, length, targets, every, 1, sems)
        send_own(z, low, length, held, every, 0, sems)
        forward(z, low, length, targets, every, 1, sems)
        forward(z, low, length, held, every, 0, sems)

    by_place(length, high, start)

    def pair(block):
        return pltpu.make_async_remote_copy(
            src_ref=leaving.at[block],
            dst_ref=coming.at[block],
            send_sem=pair_send.at[block],
            recv_sem=pair_recv.at[block],
            device_id=sibling,
            device_id_type=MESH,
        )

    def score(block):
        part = lax.dot_general(
            held[block], head_ref[...], (((1,), (1,)), ((), ())), preferred_element_type=F32
        )
        scores[block] = part
        leaving[block] = part.astype(BF16)
        pair(block).start()

    half = high // (length // 2)

    def visit(i, carry):
        side = i // length
        step = lax.rem(i, length)
        t = step + half * (length - 1 - 2 * step)
        block = t * FAST + low + side * (1 - 2 * low)
        across = at("label", high * FAST + 1 - low)

        @pl.when(side == 1)
        def _():
            hop_copy(targets, block, every, 0, 1, sems, across).wait_recv()
            hop_copy(held, block, every, 0, 0, sems, across).wait_recv()

        score(block)
        return carry

    lax.fori_loop(0, FAST * length, visit, 0)

    def finish(i, carry):
        side = i // length
        step = lax.rem(i, length)
        t = step + half * (length - 1 - 2 * step)
        block = t * FAST + low + side * (1 - 2 * low)
        pair(block).wait()
        scores[block] = scores[block] + coming[block].astype(F32)
        return carry

    lax.fori_loop(0, FAST * length, finish, 0)

    def last(z):
        wait_sent(z, low, length, targets, every, 1, sems)
        wait_sent(z, low, length, held, every, 0, sems)

    by_place(length, high, last)


def gather_score(rows, targets, head, number):
    devices = lax.axis_size("label")
    here, width = rows.shape
    labels = head.shape[0]
    if devices != 4 * FAST or lax.axis_size("tensor") != 2:
        rows = lax.all_gather(rows, "label", axis=0)
        targets = lax.all_gather(targets, "label", axis=0)
        part = jnp.einsum("nrd,jd->nrj", rows, head, preferred_element_type=F32)
        return rows, targets, lax.psum(part.astype(BF16), "tensor").astype(F32)
    return pl.pallas_call(
        functools.partial(score_kernel, devices // FAST),
        out_shape=[
            jax.ShapeDtypeStruct((devices, here, width), rows.dtype),
            jax.ShapeDtypeStruct((devices,) + targets.shape, targets.dtype),
            jax.ShapeDtypeStruct((devices, here, labels), F32),
        ],
        in_specs=[pl.BlockSpec(memory_space=pltpu.VMEM)] * 3,
        out_specs=[pl.BlockSpec(memory_space=pltpu.VMEM)] * 3,
        scratch_shapes=[pltpu.VMEM((devices, here, labels), BF16)] * 2
        + [
            pltpu.SemaphoreType.DMA((2, 3, devices)),
            pltpu.SemaphoreType.DMA((2, devices)),
            pltpu.SemaphoreType.DMA((devices,)),
            pltpu.SemaphoreType.DMA((devices,)),
        ],
        compiler_params=pltpu.CompilerParams(
            collective_id=number, has_side_effects=True, vmem_limit_bytes=VMEM_LIMIT
        ),
    )(rows, targets, head)


def weight_kernel(length, cuts, grad_ref, turned_ref, part_ref, other, held, leaving, *rest):
    send_sem, recv_sem, pair_send, pair_recv = rest
    high, low = spot()
    own = high * FAST + low
    sems = (send_sem, recv_sem)
    beside = at("dp", 1 - lax.axis_index("dp"))
    across = at("label", high * FAST + 1 - low)
    held[own] = grad_ref[...]

    def start(z):
        greet(neighbours(high, low, z, length) + [beside])
        send_own(z, low, length, held, cuts[0], 0, sems)

    def onward(part, z):
        forward(z, low, length, held, cuts[part], part, sems)
        if part + 1 < len(cuts):
            send_own(z, low, length, held, cuts[part + 1], part + 1, sems)

    def exchange(part):
        return pltpu.make_async_remote_copy(
            src_ref=leaving.at[:, cuts[part]],
            dst_ref=other.at[:, cuts[part]],
            send_sem=pair_send.at[part],
            recv_sem=pair_recv.at[part],
            device_id=beside,
            device_id_type=MESH,
        )

    by_place(length, high, start)
    for part, cols in enumerate(cuts):
        by_place(length, high, functools.partial(onward, part))
        for t in range(length):
            block = t * FAST + 1 - low
            hop_copy(held, block, cols, 0, part, sems, across).wait_recv()
        grads = held[:, :, cols]
        product = jnp.dot(
            turned_ref[...],
            grads.reshape(grads.shape[0] * grads.shape[1], grads.shape[2]),
            preferred_element_type=F32,
        )
        part_ref[:, cols] = product
        leaving[:, cols] = product.astype(BF16)
        exchange(part).start()
    for part in range(len(cuts)):
        exchange(part).wait()

    def last(z):
        for part, cols in enumerate(cuts):
            wait_sent(z, low, length, held, cols, part, sems)

    by_place(length, high, last)


def weight_grad(hidden, grad, number):
    devices = lax.axis_size("label")
    here, width = grad.shape
    features = hidden.shape[1]
    if devices != 4 * FAST or lax.axis_size("dp") != 2:
        grads = lax.all_gather(grad, "label", axis=0, tiled=True)
        return sum_over_dp(
            lax.dot_general(
                hidden, grads, (((0,), (0,)), ((), ())), preferred_element_type=F32
            )
        )
    tiles = width // 128
    pieces = min(4, tiles)
    edges = [-(-tiles * i // pieces) * 128 for i in range(pieces)] + [width]
    cuts = [slice(edges[i], edges[i + 1]) for i in range(pieces)]
    part, other = pl.pallas_call(
        functools.partial(weight_kernel, devices // FAST, cuts),
        out_shape=[
            jax.ShapeDtypeStruct((features, width), F32),
            jax.ShapeDtypeStruct((features, width), BF16),
        ],
        in_specs=[pl.BlockSpec(memory_space=pltpu.VMEM)] * 2,
        out_specs=[pl.BlockSpec(memory_space=pltpu.VMEM)] * 2,
        scratch_shapes=[
            pltpu.VMEM((devices, here, width), BF16),
            pltpu.VMEM((features, width), BF16),
            pltpu.SemaphoreType.DMA((pieces, 3, devices)),
            pltpu.SemaphoreType.DMA((pieces, devices)),
            pltpu.SemaphoreType.DMA((pieces,)),
            pltpu.SemaphoreType.DMA((pieces,)),
        ],
        compiler_params=pltpu.CompilerParams(
            collective_id=number, has_side_effects=True, vmem_limit_bytes=VMEM_LIMIT
        ),
    )(grad, hidden.T)
    return part + other.astype(F32)


def scatter_kernel(length, swap, *refs):
    if swap:
        parts, theirs, out, other = refs[:4]
        rest = refs[4:]
    else:
        parts, out = refs[:2]
        rest = refs[2:]
    crossed, in_up, in_down, out_up, out_down, send_sem, recv_sem, swap_sem = rest
    high, low = spot()
    rows = parts.shape[1]
    tile = 16

    def remote(src, dst, way, t, device):
        return pltpu.make_async_remote_copy(
            src_ref=src,
            dst_ref=dst,
            send_sem=send_sem.at[way, t],
            recv_sem=recv_sem.at[way, t],
            device_id=device,
            device_id_type=MESH,
        )

    def branch(z):
        across = at("label", z * FAST + 1 - low)
        up = at("label", (z + 1) * FAST + low)
        down = at("label", (z - 1) * FAST + low)
        greeted = neighbours(high, low, z, length)
        if swap:
            beside = at("dp", 1 - lax.axis_index("dp"))
            greeted.append(beside)
        greet(greeted)
        sent = []
        if swap:
            exchange = pltpu.make_async_remote_copy(
                src_ref=theirs,
                dst_ref=other,
                send_sem=swap_sem.at[0],
                recv_sem=swap_sem.at[1],
                device_id=beside,
                device_id_type=MESH,
            )
            exchange.start()

        order = sorted(range(length), key=lambda t: (-abs(t - z), -t))

        def cross(t):
            copy = remote(parts.at[t * FAST + 1 - low], crossed.at[t], 0, t, across)
            copy.start()
            sent.append(copy)

        def total(t, terms, result):
            def body(i, carry):
                span = pl.ds(pl.multiple_of(i * tile, tile), tile)
                value = parts[t * FAST + low, span].astype(F32) + crossed[t, span].astype(F32)
                for term in terms:
                    value += term[t, span].astype(F32)
                if result is None:
                    out[span] = value
                else:
                    result[t, span] = value.astype(BF16)
                return carry

            lax.fori_loop(0, rows // tile, body, 0)

        for t in order[:2]:
            cross(t)
        for place, t in enumerate(order):
            remote(parts.at[0], crossed.at[t], 0, t, across).wait_recv()
            if place + 2 < length:
                cross(order[place + 2])
            terms = []
            if t >= z and z > 0:
                remote(out_up.at[t], in_up.at[t], 1, t, across).wait_recv()
                terms.append(in_up)
            if t <= z and z + 1 < length:
                remote(out_down.at[t], in_down.at[t], 2, t, across).wait_recv()
                terms.append(in_down)
            if t > z:
                total(t, terms, out_up)
                copy = remote(out_up.at[t], in_up.at[t], 1, t, up)
            elif t < z:
                total(t, terms, out_down)
                copy = remote(out_down.at[t], in_down.at[t], 2, t, down)
            else:
                total(t, terms, None)
                continue
            copy.start()
            sent.append(copy)
        for copy in sent:
            copy.wait_send()
        if swap:
            exchange.wait()

    for z in range(length):
        pl.when(high == z)(functools.partial(branch, z))


def scatter_label(parts, number, theirs=None):
    devices, rows, width = parts.shape
    swap = theirs is not None
    if devices != 4 * FAST:
        out = lax.psum_scatter(parts, "label", scatter_dimension=0, tiled=False).astype(F32)
        if swap:
            return out, lax.ppermute(theirs, "dp", [(0, 1), (1, 0)])
        return out
    length = devices // FAST
    out_shape = [jax.ShapeDtypeStruct((rows, width), F32)]
    operands = [parts]
    if swap:
        out_shape.append(jax.ShapeDtypeStruct(theirs.shape, theirs.dtype))
        operands.append(theirs)
    outs = pl.pallas_call(
        functools.partial(scatter_kernel, length, swap),
        out_shape=out_shape,
        in_specs=[pl.BlockSpec(memory_space=pltpu.VMEM)] * len(operands),
        out_specs=[pl.BlockSpec(memory_space=pltpu.VMEM)] * len(operands),
        scratch_shapes=[pltpu.VMEM((length, rows, width), BF16)] * 5
        + [
            pltpu.SemaphoreType.DMA((3, length)),
            pltpu.SemaphoreType.DMA((3, length)),
            pltpu.SemaphoreType.DMA((2,)),
        ],
        compiler_params=pltpu.CompilerParams(
            collective_id=number, has_side_effects=True, vmem_limit_bytes=VMEM_LIMIT
        ),
    )(*operands)
    return outs if swap else outs[0]


def sum_over_dp(part):
    n = lax.axis_size("dp")
    if n == 2:
        other = lax.ppermute(part.astype(BF16), "dp", [(0, 1), (1, 0)])
        return part + other.astype(F32)
    return lax.psum(part.astype(BF16), "dp").astype(F32)


def shards(hidden, enc_weight, enc_gain, head_weight, propensity, blocks, offsets):
    width_half = enc_weight.shape[1]
    rows_here = blocks.shape[0]
    pos_count = offsets.shape[1]
    blocks_dev, block_size = head_weight.shape[:2]
    full_width = width_half * lax.axis_size("tensor")
    head = head_weight.reshape(blocks_dev * block_size, width_half)

    labels_n = lax.axis_size("label")
    slots = blocks.shape[1]
    targets = jnp.concatenate([blocks, offsets], axis=1).T
    targets = jnp.pad(targets, ((0, -targets.shape[0] % 8), (0, 0)))

    product = jnp.dot(hidden, enc_weight, preferred_element_type=F32).astype(BF16)
    pooled = scatter_label(product.reshape(labels_n, rows_here, width_half), 0)
    squares = lax.psum(jnp.sum(pooled * pooled, axis=1), "tensor")
    inverse = lax.rsqrt(squares / full_width + EPSILON)
    embedded = (pooled * inverse[:, None] * enc_gain[None, :]).astype(BF16)
    rows, targets, scores = gather_score(embedded, targets, head, 1)
    scores = scores.reshape(labels_n * rows_here, -1)
    rows = rows.reshape(labels_n * rows_here, width_half)
    targets = jnp.swapaxes(targets, 1, 2).reshape(labels_n * rows_here, -1)
    all_blocks, all_offsets = targets[:, :slots], targets[:, slots : slots + pos_count]

    label_ids = jnp.arange(block_size, dtype=jnp.int32)[None, :]
    first = lax.axis_index("label") * blocks_dev
    pieces = []
    for n in range(blocks_dev):
        named = all_blocks == first + n
        present = jnp.any(named, axis=1)[:, None]
        positive = jnp.zeros((), bool)
        for k in range(pos_count):
            positive = positive | (
                named[:, k : k + 1] & (all_offsets[:, k : k + 1] == label_ids)
            )
        here = scores[:, n * block_size : (n + 1) * block_size]
        weight_pos = (1.0 / propensity[n])[None, :]
        above = jnp.maximum(1.0 - here, 0.0)
        below = jnp.maximum(1.0 + here, 0.0)
        slope = jnp.where(
            positive, -2.0 * weight_pos * above + 2.0 * (1.0 - weight_pos) * below, 2.0 * below
        )
        pieces.append(jnp.where(present, slope / rows_here, 0.0).astype(BF16))
    slopes = jnp.concatenate(pieces, axis=1)

    back = jnp.dot(slopes, head, preferred_element_type=F32).astype(BF16)
    back = back.reshape(labels_n, rows_here, width_half)
    head_partial = lax.dot_general(
        slopes, rows, (((0,), (0,)), ((), ())), preferred_element_type=F32
    ).reshape(blocks_dev, block_size, width_half)
    if lax.axis_size("dp") == 2:
        half = block_size // 2
        me = lax.axis_index("dp")
        mine = lax.dynamic_slice_in_dim(head_partial, me * half, half, 1)
        theirs = lax.dynamic_slice_in_dim(head_partial, (1 - me) * half, half, 1)
        embed_grad, other = scatter_label(back, 2, theirs.astype(BF16))
        head_grad = mine + other.astype(F32)
    else:
        embed_grad = scatter_label(back, 2)
        head_grad = lax.psum_scatter(
            head_partial.astype(BF16), "dp", scatter_dimension=1, tiled=True
        ).astype(F32)

    scaled = embed_grad * enc_gain[None, :]
    row_dot = lax.psum(jnp.sum(scaled * pooled, axis=1), "tensor")
    pooled_grad = (
        inverse[:, None] * (scaled - pooled * (inverse * inverse * row_dot / full_width)[:, None])
    ).astype(BF16)
    enc_grad = weight_grad(hidden, pooled_grad, 3)
    return (enc_grad, head_grad)


def solution(mesh):
    in_specs = (
        P("dp", "label"),
        P("label", "tensor"),
        P("tensor"),
        P("label", None, "tensor"),
        P("label", None),
        P(("dp", "label"), None),
        P(("dp", "label"), None),
    )
    out_specs = (P("label", "tensor"), P("label", "dp", "tensor"))
    return jax.shard_map(shards, mesh=mesh, in_specs=in_specs, out_specs=out_specs, check_vma=False)
```

```python
import functools

import jax
import jax.numpy as jnp
from jax import lax
from jax.experimental import pallas as pl
from jax.experimental.pallas import tpu as pltpu
from jax.sharding import PartitionSpec as P

EPSILON = 1e-06
F32 = jnp.float32
BF16 = jnp.bfloat16


MESH = pl.DeviceIdType.MESH
FAST = 2
VMEM_LIMIT = 40 * 1024 * 1024


def spot():
    me = lax.axis_index("label")
    return me // FAST, lax.rem(me, FAST)


def at(axis, index):
    here = {name: lax.axis_index(name) for name in ("dp", "label", "tensor")}
    here[axis] = index
    return (here["dp"], here["label"], here["tensor"])


def greet(devices):
    barrier = pltpu.get_barrier_semaphore()
    for device in devices:
        pl.semaphore_signal(barrier, inc=1, device_id=device, device_id_type=MESH)
    pl.semaphore_wait(barrier, len(devices))


def neighbours(high, low, z, length):
    found = [at("label", z * FAST + 1 - low)]
    if z + 1 < length:
        found.append(at("label", (z + 1) * FAST + low))
    if z > 0:
        found.append(at("label", (z - 1) * FAST + low))
    return found


def hop_copy(held, block, cols, way, part, sems, device):
    send_sem, recv_sem = sems
    return pltpu.make_async_remote_copy(
        src_ref=held.at[block, :, cols],
        dst_ref=held.at[block, :, cols],
        send_sem=send_sem.at[part, way, block],
        recv_sem=recv_sem.at[part, block],
        device_id=device,
        device_id_type=MESH,
    )


def devices_of(z, low):
    return (
        at("label", z * FAST + 1 - low),
        at("label", (z + 1) * FAST + low),
        at("label", (z - 1) * FAST + low),
    )


def send_own(z, low, length, held, cols, part, sems):
    own = z * FAST + low
    across, up, down = devices_of(z, low)
    if z + 1 < length:
        hop_copy(held, own, cols, 1, part, sems, up).start()
    if z > 0:
        hop_copy(held, own, cols, 2, part, sems, down).start()
    hop_copy(held, own, cols, 0, part, sems, across).start()


def forward(z, low, length, held, cols, part, sems):
    across, up, down = devices_of(z, low)
    for step in range(1, length):
        if z - step >= 0:
            block = (z - step) * FAST + low
            hop_copy(held, block, cols, 0, part, sems, across).wait_recv()
            if z + 1 < length:
                hop_copy(held, block, cols, 1, part, sems, up).start()
            hop_copy(held, block, cols, 0, part, sems, across).start()
        if z + step < length:
            block = (z + step) * FAST + low
            hop_copy(held, block, cols, 0, part, sems, across).wait_recv()
            if z > 0:
                hop_copy(held, block, cols, 2, part, sems, down).start()
            hop_copy(held, block, cols, 0, part, sems, across).start()


def wait_sent(z, low, length, held, cols, part, sems):
    across, up, down = devices_of(z, low)
    for t in range(length):
        block = t * FAST + low
        hop_copy(held, block, cols, 0, part, sems, across).wait_send()
        if t <= z and z + 1 < length:
            hop_copy(held, block, cols, 1, part, sems, up).wait_send()
        if t >= z and z > 0:
            hop_copy(held, block, cols, 2, part, sems, down).wait_send()


def by_place(length, high, body):
    for z in range(length):
        pl.when(high == z)(functools.partial(body, z))


def score_kernel(length, rows_ref, target_ref, head_ref, held, targets, scores, *rest):
    leaving, coming, send_sem, recv_sem, pair_send, pair_recv = rest
    high, low = spot()
    own = high * FAST + low
    every = slice(None)
    sems = (send_sem, recv_sem)
    sibling = at("tensor", 1 - lax.axis_index("tensor"))
    held[own] = rows_ref[...]
    targets[own] = target_ref[...]

    def start(z):
        greet(neighbours(high, low, z, length) + [sibling])
        send_own(z, low, length, targets, every, 1, sems)
        send_own(z, low, length, held, every, 0, sems)
        forward(z, low, length, targets, every, 1, sems)
        forward(z, low, length, held, every, 0, sems)

    by_place(length, high, start)

    def pair(block):
        return pltpu.make_async_remote_copy(
            src_ref=leaving.at[block],
            dst_ref=coming.at[block],
            send_sem=pair_send.at[block],
            recv_sem=pair_recv.at[block],
            device_id=sibling,
            device_id_type=MESH,
        )

    def score(block):
        part = lax.dot_general(
            held[block], head_ref[...], (((1,), (1,)), ((), ())), preferred_element_type=F32
        )
        scores[block] = part
        leaving[block] = part.astype(BF16)
        pair(block).start()

    half = high // (length // 2)

    def visit(i, carry):
        side = i // length
        step = lax.rem(i, length)
        t = step + half * (length - 1 - 2 * step)
        block = t * FAST + low + side * (1 - 2 * low)
        across = at("label", high * FAST + 1 - low)

        @pl.when(side == 1)
        def _():
            hop_copy(targets, block, every, 0, 1, sems, across).wait_recv()
            hop_copy(held, block, every, 0, 0, sems, across).wait_recv()

        score(block)
        return carry

    lax.fori_loop(0, FAST * length, visit, 0)

    def finish(i, carry):
        side = i // length
        step = lax.rem(i, length)
        t = step + half * (length - 1 - 2 * step)
        block = t * FAST + low + side * (1 - 2 * low)
        pair(block).wait()
        scores[block] = scores[block] + coming[block].astype(F32)
        return carry

    lax.fori_loop(0, FAST * length, finish, 0)

    def last(z):
        wait_sent(z, low, length, targets, every, 1, sems)
        wait_sent(z, low, length, held, every, 0, sems)

    by_place(length, high, last)


def gather_score(rows, targets, head, number):
    devices = lax.axis_size("label")
    here, width = rows.shape
    labels = head.shape[0]
    if devices != 4 * FAST or lax.axis_size("tensor") != 2:
        rows = lax.all_gather(rows, "label", axis=0)
        targets = lax.all_gather(targets, "label", axis=0)
        part = jnp.einsum("nrd,jd->nrj", rows, head, preferred_element_type=F32)
        return rows, targets, lax.psum(part.astype(BF16), "tensor").astype(F32)
    return pl.pallas_call(
        functools.partial(score_kernel, devices // FAST),
        out_shape=[
            jax.ShapeDtypeStruct((devices, here, width), rows.dtype),
            jax.ShapeDtypeStruct((devices,) + targets.shape, targets.dtype),
            jax.ShapeDtypeStruct((devices, here, labels), F32),
        ],
        in_specs=[pl.BlockSpec(memory_space=pltpu.VMEM)] * 3,
        out_specs=[pl.BlockSpec(memory_space=pltpu.VMEM)] * 3,
        scratch_shapes=[pltpu.VMEM((devices, here, labels), BF16)] * 2
        + [
            pltpu.SemaphoreType.DMA((2, 3, devices)),
            pltpu.SemaphoreType.DMA((2, devices)),
            pltpu.SemaphoreType.DMA((devices,)),
            pltpu.SemaphoreType.DMA((devices,)),
        ],
        compiler_params=pltpu.CompilerParams(
            collective_id=number, has_side_effects=True, vmem_limit_bytes=VMEM_LIMIT
        ),
    )(rows, targets, head)


def weight_kernel(length, cuts, grad_ref, turned_ref, part_ref, other, held, leaving, *rest):
    send_sem, recv_sem, pair_send, pair_recv = rest
    high, low = spot()
    own = high * FAST + low
    sems = (send_sem, recv_sem)
    beside = at("dp", 1 - lax.axis_index("dp"))
    across = at("label", high * FAST + 1 - low)
    held[own] = grad_ref[...]

    def start(z):
        greet(neighbours(high, low, z, length) + [beside])
        send_own(z, low, length, held, cuts[0], 0, sems)

    def onward(part, z):
        if part > 0:
            send_own(z, low, length, held, cuts[part], part, sems)
        forward(z, low, length, held, cuts[part], part, sems)

    def exchange(part):
        return pltpu.make_async_remote_copy(
            src_ref=leaving.at[:, cuts[part]],
            dst_ref=other.at[:, cuts[part]],
            send_sem=pair_send.at[part],
            recv_sem=pair_recv.at[part],
            device_id=beside,
            device_id_type=MESH,
        )

    by_place(length, high, start)
    by_place(length, high, functools.partial(onward, 0))
    for part, cols in enumerate(cuts):
        if part + 1 < len(cuts):
            by_place(length, high, functools.partial(onward, part + 1))
        for t in range(length):
            block = t * FAST + 1 - low
            hop_copy(held, block, cols, 0, part, sems, across).wait_recv()
        grads = held[:, :, cols]
        product = jnp.dot(
            turned_ref[...],
            grads.reshape(grads.shape[0] * grads.shape[1], grads.shape[2]),
            preferred_element_type=F32,
        )
        part_ref[:, cols] = product
        leaving[:, cols] = product.astype(BF16)
        exchange(part).start()
    for part in range(len(cuts)):
        exchange(part).wait()

    def last(z):
        for part, cols in enumerate(cuts):
            wait_sent(z, low, length, held, cols, part, sems)

    by_place(length, high, last)


def weight_grad(hidden, grad, number):
    devices = lax.axis_size("label")
    here, width = grad.shape
    features = hidden.shape[1]
    if devices != 4 * FAST or lax.axis_size("dp") != 2:
        grads = lax.all_gather(grad, "label", axis=0, tiled=True)
        return sum_over_dp(
            lax.dot_general(
                hidden, grads, (((0,), (0,)), ((), ())), preferred_element_type=F32
            )
        )
    tiles = width // 128
    pieces = min(4, tiles)
    edges = [-(-tiles * i // pieces) * 128 for i in range(pieces)] + [width]
    cuts = [slice(edges[i], edges[i + 1]) for i in range(pieces)]
    part, other = pl.pallas_call(
        functools.partial(weight_kernel, devices // FAST, cuts),
        out_shape=[
            jax.ShapeDtypeStruct((features, width), F32),
            jax.ShapeDtypeStruct((features, width), BF16),
        ],
        in_specs=[pl.BlockSpec(memory_space=pltpu.VMEM)] * 2,
        out_specs=[pl.BlockSpec(memory_space=pltpu.VMEM)] * 2,
        scratch_shapes=[
            pltpu.VMEM((devices, here, width), BF16),
            pltpu.VMEM((features, width), BF16),
            pltpu.SemaphoreType.DMA((pieces, 3, devices)),
            pltpu.SemaphoreType.DMA((pieces, devices)),
            pltpu.SemaphoreType.DMA((pieces,)),
            pltpu.SemaphoreType.DMA((pieces,)),
        ],
        compiler_params=pltpu.CompilerParams(
            collective_id=number, has_side_effects=True, vmem_limit_bytes=VMEM_LIMIT
        ),
    )(grad, hidden.T)
    return part + other.astype(F32)


def scatter_kernel(length, swap, *refs):
    if swap:
        parts, slopes, rows_ref, out, mine, other, theirs = refs[:7]
        rest = refs[7:]
    else:
        parts, out = refs[:2]
        rest = refs[2:]
    crossed, in_up, in_down, out_up, out_down, send_sem, recv_sem, swap_sem = rest
    high, low = spot()
    rows = parts.shape[1]
    tile = 16

    def remote(src, dst, way, t, device):
        return pltpu.make_async_remote_copy(
            src_ref=src,
            dst_ref=dst,
            send_sem=send_sem.at[way, t],
            recv_sem=recv_sem.at[way, t],
            device_id=device,
            device_id_type=MESH,
        )

    if swap:
        me = lax.axis_index("dp")
        exchange = pltpu.make_async_remote_copy(
            src_ref=theirs,
            dst_ref=other,
            send_sem=swap_sem.at[0],
            recv_sem=swap_sem.at[1],
            device_id=at("dp", 1 - me),
            device_id_type=MESH,
        )

    def order_of(z):
        return sorted(range(length), key=lambda t: (-abs(t - z), -t))

    def crossing(z, t):
        across = at("label", z * FAST + 1 - low)
        return remote(parts.at[t * FAST + 1 - low], crossed.at[t], 0, t, across)

    def begin(z):
        greeted = neighbours(high, low, z, length)
        if swap:
            greeted.append(at("dp", 1 - me))
        greet(greeted)
        for t in order_of(z)[:2]:
            crossing(z, t).start()

    def head_products():
        count, half = theirs.shape[:2]

        def product(n, side):
            span = pl.ds(pl.multiple_of((n * 2 + side) * half, half), half)
            return lax.dot_general(
                slopes[:, span],
                rows_ref[...],
                (((0,), (0,)), ((), ())),
                preferred_element_type=F32,
            )

        def for_other(n, carry):
            theirs[n] = product(n, 1 - me).astype(BF16)
            return carry

        def for_own(n, carry):
            mine[n] = product(n, me)
            return carry

        lax.fori_loop(0, count, for_other, 0)
        exchange.start()
        lax.fori_loop(0, count, for_own, 0)

    def branch(z):
        across = at("label", z * FAST + 1 - low)
        up = at("label", (z + 1) * FAST + low)
        down = at("label", (z - 1) * FAST + low)
        order = order_of(z)
        sent = [crossing(z, t) for t in order[:2]]

        def cross(t):
            copy = crossing(z, t)
            copy.start()
            sent.append(copy)

        def total(t, terms, result):
            def body(i, carry):
                span = pl.ds(pl.multiple_of(i * tile, tile), tile)
                value = parts[t * FAST + low, span].astype(F32) + crossed[t, span].astype(F32)
                for term in terms:
                    value += term[t, span].astype(F32)
                if result is None:
                    out[span] = value
                else:
                    result[t, span] = value.astype(BF16)
                return carry

            lax.fori_loop(0, rows // tile, body, 0)

        for place, t in enumerate(order):
            remote(parts.at[0], crossed.at[t], 0, t, across).wait_recv()
            if place + 2 < length:
                cross(order[place + 2])
            terms = []
            if t >= z and z > 0:
                remote(out_up.at[t], in_up.at[t], 1, t, across).wait_recv()
                terms.append(in_up)
            if t <= z and z + 1 < length:
                remote(out_down.at[t], in_down.at[t], 2, t, across).wait_recv()
                terms.append(in_down)
            if t > z:
                total(t, terms, out_up)
                copy = remote(out_up.at[t], in_up.at[t], 1, t, up)
            elif t < z:
                total(t, terms, out_down)
                copy = remote(out_down.at[t], in_down.at[t], 2, t, down)
            else:
                total(t, terms, None)
                continue
            copy.start()
            sent.append(copy)
        for copy in sent:
            copy.wait_send()

    by_place(length, high, begin)
    if swap:
        head_products()
    by_place(length, high, branch)
    if swap:
        exchange.wait()


def scatter_label(parts, number, slopes=None, rows=None, count=0):
    devices, here, width = parts.shape
    swap = slopes is not None
    if devices != 4 * FAST or (swap and lax.axis_size("dp") != 2):
        out = lax.psum_scatter(parts, "label", scatter_dimension=0, tiled=False).astype(F32)
        if not swap:
            return out
        whole = lax.dot_general(
            slopes, rows, (((0,), (0,)), ((), ())), preferred_element_type=F32
        ).reshape(count, -1, width)
        whole = lax.psum_scatter(whole.astype(BF16), "dp", scatter_dimension=1, tiled=True)
        return out, whole.astype(F32)
    length = devices // FAST
    out_shape = [jax.ShapeDtypeStruct((here, width), F32)]
    operands = [parts]
    scratch = []
    if swap:
        share = (count, slopes.shape[1] // count // 2, width)
        out_shape += [jax.ShapeDtypeStruct(share, F32), jax.ShapeDtypeStruct(share, BF16)]
        operands += [slopes, rows]
        scratch = [pltpu.VMEM(share, BF16)]
    outs = pl.pallas_call(
        functools.partial(scatter_kernel, length, swap),
        out_shape=out_shape,
        in_specs=[pl.BlockSpec(memory_space=pltpu.VMEM)] * len(operands),
        out_specs=[pl.BlockSpec(memory_space=pltpu.VMEM)] * len(out_shape),
        scratch_shapes=scratch
        + [pltpu.VMEM((length, here, width), BF16)] * 5
        + [
            pltpu.SemaphoreType.DMA((3, length)),
            pltpu.SemaphoreType.DMA((3, length)),
            pltpu.SemaphoreType.DMA((2,)),
        ],
        compiler_params=pltpu.CompilerParams(
            collective_id=number, has_side_effects=True, vmem_limit_bytes=VMEM_LIMIT
        ),
    )(*operands)
    if not swap:
        return outs[0]
    return outs[0], outs[1] + outs[2].astype(F32)


def sum_over_dp(part):
    n = lax.axis_size("dp")
    if n == 2:
        other = lax.ppermute(part.astype(BF16), "dp", [(0, 1), (1, 0)])
        return part + other.astype(F32)
    return lax.psum(part.astype(BF16), "dp").astype(F32)


def shards(hidden, enc_weight, enc_gain, head_weight, propensity, blocks, offsets):
    width_half = enc_weight.shape[1]
    rows_here = blocks.shape[0]
    pos_count = offsets.shape[1]
    blocks_dev, block_size = head_weight.shape[:2]
    full_width = width_half * lax.axis_size("tensor")
    head = head_weight.reshape(blocks_dev * block_size, width_half)

    labels_n = lax.axis_size("label")
    slots = blocks.shape[1]
    targets = jnp.concatenate([blocks, offsets], axis=1).T
    targets = jnp.pad(targets, ((0, -targets.shape[0] % 8), (0, 0)))

    product = jnp.dot(hidden, enc_weight, preferred_element_type=F32).astype(BF16)
    pooled = scatter_label(product.reshape(labels_n, rows_here, width_half), 0)
    squares = lax.psum(jnp.sum(pooled * pooled, axis=1), "tensor")
    inverse = lax.rsqrt(squares / full_width + EPSILON)
    embedded = (pooled * inverse[:, None] * enc_gain[None, :]).astype(BF16)
    rows, targets, scores = gather_score(embedded, targets, head, 1)
    scores = scores.reshape(labels_n * rows_here, -1)
    rows = rows.reshape(labels_n * rows_here, width_half)
    targets = jnp.swapaxes(targets, 1, 2).reshape(labels_n * rows_here, -1)
    all_blocks, all_offsets = targets[:, :slots], targets[:, slots : slots + pos_count]

    label_ids = jnp.arange(block_size, dtype=jnp.int32)[None, :]
    first = lax.axis_index("label") * blocks_dev
    pieces = []
    for n in range(blocks_dev):
        named = all_blocks == first + n
        present = jnp.any(named, axis=1)[:, None]
        positive = jnp.zeros((), bool)
        for k in range(pos_count):
            positive = positive | (
                named[:, k : k + 1] & (all_offsets[:, k : k + 1] == label_ids)
            )
        here = scores[:, n * block_size : (n + 1) * block_size]
        weight_pos = (1.0 / propensity[n])[None, :]
        above = jnp.maximum(1.0 - here, 0.0)
        below = jnp.maximum(1.0 + here, 0.0)
        slope = jnp.where(
            positive, -2.0 * weight_pos * above + 2.0 * (1.0 - weight_pos) * below, 2.0 * below
        )
        pieces.append(jnp.where(present, slope / rows_here, 0.0).astype(BF16))
    slopes = jnp.concatenate(pieces, axis=1)

    back = jnp.dot(slopes, head, preferred_element_type=F32).astype(BF16)
    back = back.reshape(labels_n, rows_here, width_half)
    embed_grad, head_grad = scatter_label(back, 2, slopes, rows, blocks_dev)

    scaled = embed_grad * enc_gain[None, :]
    row_dot = lax.psum(jnp.sum(scaled * pooled, axis=1), "tensor")
    pooled_grad = (
        inverse[:, None] * (scaled - pooled * (inverse * inverse * row_dot / full_width)[:, None])
    ).astype(BF16)
    enc_grad = weight_grad(hidden, pooled_grad, 3)
    return (enc_grad, head_grad)


def solution(mesh):
    in_specs = (
        P("dp", "label"),
        P("label", "tensor"),
        P("tensor"),
        P("label", None, "tensor"),
        P("label", None),
        P(("dp", "label"), None),
        P(("dp", "label"), None),
    )
    out_specs = (P("label", "tensor"), P("label", "dp", "tensor"))
    return jax.shard_map(shards, mesh=mesh, in_specs=in_specs, out_specs=out_specs, check_vma=False)
```

```python
import functools

import jax
import jax.numpy as jnp
from jax import lax
from jax.experimental import pallas as pl
from jax.experimental.pallas import tpu as pltpu
from jax.sharding import PartitionSpec as P

EPSILON = 1e-06
F32 = jnp.float32
BF16 = jnp.bfloat16


MESH = pl.DeviceIdType.MESH
FAST = 2
VMEM_LIMIT = 40 * 1024 * 1024


def spot():
    me = lax.axis_index("label")
    return me // FAST, lax.rem(me, FAST)


def at(axis, index):
    here = {name: lax.axis_index(name) for name in ("dp", "label", "tensor")}
    here[axis] = index
    return (here["dp"], here["label"], here["tensor"])


def greet(devices):
    barrier = pltpu.get_barrier_semaphore()
    for device in devices:
        pl.semaphore_signal(barrier, inc=1, device_id=device, device_id_type=MESH)
    pl.semaphore_wait(barrier, len(devices))


def neighbours(high, low, z, length):
    found = [at("label", z * FAST + 1 - low)]
    if z + 1 < length:
        found.append(at("label", (z + 1) * FAST + low))
    if z > 0:
        found.append(at("label", (z - 1) * FAST + low))
    return found


def hop_copy(held, block, cols, way, part, sems, device):
    send_sem, recv_sem = sems
    return pltpu.make_async_remote_copy(
        src_ref=held.at[block, :, cols],
        dst_ref=held.at[block, :, cols],
        send_sem=send_sem.at[part, way, block],
        recv_sem=recv_sem.at[part, block],
        device_id=device,
        device_id_type=MESH,
    )


def devices_of(z, low):
    return (
        at("label", z * FAST + 1 - low),
        at("label", (z + 1) * FAST + low),
        at("label", (z - 1) * FAST + low),
    )


def send_own(z, low, length, held, cols, part, sems):
    own = z * FAST + low
    across, up, down = devices_of(z, low)
    if z + 1 < length:
        hop_copy(held, own, cols, 1, part, sems, up).start()
    if z > 0:
        hop_copy(held, own, cols, 2, part, sems, down).start()
    hop_copy(held, own, cols, 0, part, sems, across).start()


def forward(z, low, length, held, cols, part, sems):
    across, up, down = devices_of(z, low)
    for step in range(1, length):
        if z - step >= 0:
            block = (z - step) * FAST + low
            hop_copy(held, block, cols, 0, part, sems, across).wait_recv()
            if z + 1 < length:
                hop_copy(held, block, cols, 1, part, sems, up).start()
            hop_copy(held, block, cols, 0, part, sems, across).start()
        if z + step < length:
            block = (z + step) * FAST + low
            hop_copy(held, block, cols, 0, part, sems, across).wait_recv()
            if z > 0:
                hop_copy(held, block, cols, 2, part, sems, down).start()
            hop_copy(held, block, cols, 0, part, sems, across).start()


def wait_sent(z, low, length, held, cols, part, sems):
    across, up, down = devices_of(z, low)
    for t in range(length):
        block = t * FAST + low
        hop_copy(held, block, cols, 0, part, sems, across).wait_send()
        if t <= z and z + 1 < length:
            hop_copy(held, block, cols, 1, part, sems, up).wait_send()
        if t >= z and z > 0:
            hop_copy(held, block, cols, 2, part, sems, down).wait_send()


def by_place(length, high, body):
    for z in range(length):
        pl.when(high == z)(functools.partial(body, z))


def score_kernel(length, rows_ref, target_ref, head_ref, held, targets, scores, *rest):
    leaving, coming, send_sem, recv_sem, pair_send, pair_recv = rest
    high, low = spot()
    own = high * FAST + low
    every = slice(None)
    sems = (send_sem, recv_sem)
    sibling = at("tensor", 1 - lax.axis_index("tensor"))
    held[own] = rows_ref[...]
    targets[own] = target_ref[...]

    def start(z):
        greet(neighbours(high, low, z, length) + [sibling])
        send_own(z, low, length, targets, every, 1, sems)
        send_own(z, low, length, held, every, 0, sems)
        forward(z, low, length, held, every, 0, sems)
        forward(z, low, length, targets, every, 1, sems)

    by_place(length, high, start)

    def pair(block):
        return pltpu.make_async_remote_copy(
            src_ref=leaving.at[block],
            dst_ref=coming.at[block],
            send_sem=pair_send.at[block],
            recv_sem=pair_recv.at[block],
            device_id=sibling,
            device_id_type=MESH,
        )

    def score(block):
        part = lax.dot_general(
            held[block], head_ref[...], (((1,), (1,)), ((), ())), preferred_element_type=F32
        )
        scores[block] = part
        leaving[block] = part.astype(BF16)
        pair(block).start()

    half = high // (length // 2)

    def visit(i, carry):
        side = i // length
        step = lax.rem(i, length)
        t = step + half * (length - 1 - 2 * step)
        block = t * FAST + low + side * (1 - 2 * low)
        across = at("label", high * FAST + 1 - low)

        @pl.when(side == 1)
        def _():
            hop_copy(targets, block, every, 0, 1, sems, across).wait_recv()
            hop_copy(held, block, every, 0, 0, sems, across).wait_recv()

        score(block)
        return carry

    lax.fori_loop(0, FAST * length, visit, 0)

    def finish(i, carry):
        side = i // length
        step = lax.rem(i, length)
        t = step + half * (length - 1 - 2 * step)
        block = t * FAST + low + side * (1 - 2 * low)
        pair(block).wait()
        scores[block] = scores[block] + coming[block].astype(F32)
        return carry

    lax.fori_loop(0, FAST * length, finish, 0)

    def last(z):
        wait_sent(z, low, length, targets, every, 1, sems)
        wait_sent(z, low, length, held, every, 0, sems)

    by_place(length, high, last)


def gather_score(rows, targets, head, number):
    devices = lax.axis_size("label")
    here, width = rows.shape
    labels = head.shape[0]
    if devices != 4 * FAST or lax.axis_size("tensor") != 2:
        rows = lax.all_gather(rows, "label", axis=0)
        targets = lax.all_gather(targets, "label", axis=0)
        part = jnp.einsum("nrd,jd->nrj", rows, head, preferred_element_type=F32)
        return rows, targets, lax.psum(part.astype(BF16), "tensor").astype(F32)
    return pl.pallas_call(
        functools.partial(score_kernel, devices // FAST),
        out_shape=[
            jax.ShapeDtypeStruct((devices, here, width), rows.dtype),
            jax.ShapeDtypeStruct((devices,) + targets.shape, targets.dtype),
            jax.ShapeDtypeStruct((devices, here, labels), F32),
        ],
        in_specs=[pl.BlockSpec(memory_space=pltpu.VMEM)] * 3,
        out_specs=[pl.BlockSpec(memory_space=pltpu.VMEM)] * 3,
        scratch_shapes=[pltpu.VMEM((devices, here, labels), BF16)] * 2
        + [
            pltpu.SemaphoreType.DMA((2, 3, devices)),
            pltpu.SemaphoreType.DMA((2, devices)),
            pltpu.SemaphoreType.DMA((devices,)),
            pltpu.SemaphoreType.DMA((devices,)),
        ],
        compiler_params=pltpu.CompilerParams(
            collective_id=number, has_side_effects=True, vmem_limit_bytes=VMEM_LIMIT
        ),
    )(rows, targets, head)


def weight_kernel(length, cuts, grad_ref, turned_ref, part_ref, other, held, leaving, *rest):
    send_sem, recv_sem, pair_send, pair_recv = rest
    high, low = spot()
    own = high * FAST + low
    sems = (send_sem, recv_sem)
    beside = at("dp", 1 - lax.axis_index("dp"))
    across = at("label", high * FAST + 1 - low)
    held[own] = grad_ref[...]

    def start(z):
        greet(neighbours(high, low, z, length) + [beside])
        send_own(z, low, length, held, cuts[0], 0, sems)

    def onward(part, z):
        forward(z, low, length, held, cuts[part], part, sems)
        if part + 1 < len(cuts):
            send_own(z, low, length, held, cuts[part + 1], part + 1, sems)

    def exchange(part):
        return pltpu.make_async_remote_copy(
            src_ref=leaving.at[:, cuts[part]],
            dst_ref=other.at[:, cuts[part]],
            send_sem=pair_send.at[part],
            recv_sem=pair_recv.at[part],
            device_id=beside,
            device_id_type=MESH,
        )

    by_place(length, high, start)
    for part, cols in enumerate(cuts):
        by_place(length, high, functools.partial(onward, part))
        for t in range(length):
            block = t * FAST + 1 - low
            hop_copy(held, block, cols, 0, part, sems, across).wait_recv()
        grads = held[:, :, cols]
        product = jnp.dot(
            turned_ref[...],
            grads.reshape(grads.shape[0] * grads.shape[1], grads.shape[2]),
            preferred_element_type=F32,
        )
        part_ref[:, cols] = product
        leaving[:, cols] = product.astype(BF16)
        exchange(part).start()
    for part in range(len(cuts)):
        exchange(part).wait()

    def last(z):
        for part, cols in enumerate(cuts):
            wait_sent(z, low, length, held, cols, part, sems)

    by_place(length, high, last)


def weight_grad(hidden, grad, number):
    devices = lax.axis_size("label")
    here, width = grad.shape
    features = hidden.shape[1]
    if devices != 4 * FAST or lax.axis_size("dp") != 2:
        grads = lax.all_gather(grad, "label", axis=0, tiled=True)
        return sum_over_dp(
            lax.dot_general(
                hidden, grads, (((0,), (0,)), ((), ())), preferred_element_type=F32
            )
        )
    tiles = width // 128
    pieces = min(3, tiles)
    edges = [-(-tiles * i // pieces) * 128 for i in range(pieces)] + [width]
    cuts = [slice(edges[i], edges[i + 1]) for i in range(pieces)]
    part, other = pl.pallas_call(
        functools.partial(weight_kernel, devices // FAST, cuts),
        out_shape=[
            jax.ShapeDtypeStruct((features, width), F32),
            jax.ShapeDtypeStruct((features, width), BF16),
        ],
        in_specs=[pl.BlockSpec(memory_space=pltpu.VMEM)] * 2,
        out_specs=[pl.BlockSpec(memory_space=pltpu.VMEM)] * 2,
        scratch_shapes=[
            pltpu.VMEM((devices, here, width), BF16),
            pltpu.VMEM((features, width), BF16),
            pltpu.SemaphoreType.DMA((pieces, 3, devices)),
            pltpu.SemaphoreType.DMA((pieces, devices)),
            pltpu.SemaphoreType.DMA((pieces,)),
            pltpu.SemaphoreType.DMA((pieces,)),
        ],
        compiler_params=pltpu.CompilerParams(
            collective_id=number, has_side_effects=True, vmem_limit_bytes=VMEM_LIMIT
        ),
    )(grad, hidden.T)
    return part + other.astype(F32)


def scatter_kernel(length, swap, *refs):
    if swap:
        parts, slopes, rows_ref, out, mine, other, theirs = refs[:7]
        rest = refs[7:]
    else:
        parts, out = refs[:2]
        rest = refs[2:]
    crossed, in_up, in_down, out_up, out_down, send_sem, recv_sem, swap_sem = rest
    high, low = spot()
    rows = parts.shape[1]
    tile = 16

    def remote(src, dst, way, t, device):
        return pltpu.make_async_remote_copy(
            src_ref=src,
            dst_ref=dst,
            send_sem=send_sem.at[way, t],
            recv_sem=recv_sem.at[way, t],
            device_id=device,
            device_id_type=MESH,
        )

    if swap:
        me = lax.axis_index("dp")
        exchange = pltpu.make_async_remote_copy(
            src_ref=theirs,
            dst_ref=other,
            send_sem=swap_sem.at[0],
            recv_sem=swap_sem.at[1],
            device_id=at("dp", 1 - me),
            device_id_type=MESH,
        )

    def order_of(z):
        return sorted(range(length), key=lambda t: (-abs(t - z), -t))

    def crossing(z, t):
        across = at("label", z * FAST + 1 - low)
        return remote(parts.at[t * FAST + 1 - low], crossed.at[t], 0, t, across)

    def begin(z):
        greeted = neighbours(high, low, z, length)
        if swap:
            greeted.append(at("dp", 1 - me))
        greet(greeted)
        for t in order_of(z)[:2]:
            crossing(z, t).start()

    def head_products():
        count, half = theirs.shape[:2]

        def product(n, side):
            span = pl.ds(pl.multiple_of((n * 2 + side) * half, half), half)
            return lax.dot_general(
                slopes[:, span],
                rows_ref[...],
                (((0,), (0,)), ((), ())),
                preferred_element_type=F32,
            )

        def for_other(n, carry):
            theirs[n] = product(n, 1 - me).astype(BF16)
            return carry

        def for_own(n, carry):
            mine[n] = product(n, me)
            return carry

        lax.fori_loop(0, count, for_other, 0)
        exchange.start()
        lax.fori_loop(0, count, for_own, 0)

    def branch(z):
        across = at("label", z * FAST + 1 - low)
        up = at("label", (z + 1) * FAST + low)
        down = at("label", (z - 1) * FAST + low)
        order = order_of(z)
        sent = [crossing(z, t) for t in order[:2]]

        def cross(t):
            copy = crossing(z, t)
            copy.start()
            sent.append(copy)

        def total(t, terms, result):
            def body(i, carry):
                span = pl.ds(pl.multiple_of(i * tile, tile), tile)
                value = parts[t * FAST + low, span].astype(F32) + crossed[t, span].astype(F32)
                for term in terms:
                    value += term[t, span].astype(F32)
                if result is None:
                    out[span] = value
                else:
                    result[t, span] = value.astype(BF16)
                return carry

            lax.fori_loop(0, rows // tile, body, 0)

        for place, t in enumerate(order):
            remote(parts.at[0], crossed.at[t], 0, t, across).wait_recv()
            if place + 2 < length:
                cross(order[place + 2])
            terms = []
            if t >= z and z > 0:
                remote(out_up.at[t], in_up.at[t], 1, t, across).wait_recv()
                terms.append(in_up)
            if t <= z and z + 1 < length:
                remote(out_down.at[t], in_down.at[t], 2, t, across).wait_recv()
                terms.append(in_down)
            if t > z:
                total(t, terms, out_up)
                copy = remote(out_up.at[t], in_up.at[t], 1, t, up)
            elif t < z:
                total(t, terms, out_down)
                copy = remote(out_down.at[t], in_down.at[t], 2, t, down)
            else:
                total(t, terms, None)
                continue
            copy.start()
            sent.append(copy)
        for copy in sent:
            copy.wait_send()

    by_place(length, high, begin)
    if swap:
        head_products()
    by_place(length, high, branch)
    if swap:
        exchange.wait()


def scatter_label(parts, number, slopes=None, rows=None, count=0):
    devices, here, width = parts.shape
    swap = slopes is not None
    if devices != 4 * FAST or (swap and lax.axis_size("dp") != 2):
        out = lax.psum_scatter(parts, "label", scatter_dimension=0, tiled=False).astype(F32)
        if not swap:
            return out
        whole = lax.dot_general(
            slopes, rows, (((0,), (0,)), ((), ())), preferred_element_type=F32
        ).reshape(count, -1, width)
        whole = lax.psum_scatter(whole.astype(BF16), "dp", scatter_dimension=1, tiled=True)
        return out, whole.astype(F32)
    length = devices // FAST
    out_shape = [jax.ShapeDtypeStruct((here, width), F32)]
    operands = [parts]
    scratch = []
    if swap:
        share = (count, slopes.shape[1] // count // 2, width)
        out_shape += [jax.ShapeDtypeStruct(share, F32), jax.ShapeDtypeStruct(share, BF16)]
        operands += [slopes, rows]
        scratch = [pltpu.VMEM(share, BF16)]
    outs = pl.pallas_call(
        functools.partial(scatter_kernel, length, swap),
        out_shape=out_shape,
        in_specs=[pl.BlockSpec(memory_space=pltpu.VMEM)] * len(operands),
        out_specs=[pl.BlockSpec(memory_space=pltpu.VMEM)] * len(out_shape),
        scratch_shapes=scratch
        + [pltpu.VMEM((length, here, width), BF16)] * 5
        + [
            pltpu.SemaphoreType.DMA((3, length)),
            pltpu.SemaphoreType.DMA((3, length)),
            pltpu.SemaphoreType.DMA((2,)),
        ],
        compiler_params=pltpu.CompilerParams(
            collective_id=number, has_side_effects=True, vmem_limit_bytes=VMEM_LIMIT
        ),
    )(*operands)
    if not swap:
        return outs[0]
    return outs[0], outs[1] + outs[2].astype(F32)


def sum_over_dp(part):
    n = lax.axis_size("dp")
    if n == 2:
        other = lax.ppermute(part.astype(BF16), "dp", [(0, 1), (1, 0)])
        return part + other.astype(F32)
    return lax.psum(part.astype(BF16), "dp").astype(F32)


def shards(hidden, enc_weight, enc_gain, head_weight, propensity, blocks, offsets):
    width_half = enc_weight.shape[1]
    rows_here = blocks.shape[0]
    pos_count = offsets.shape[1]
    blocks_dev, block_size = head_weight.shape[:2]
    full_width = width_half * lax.axis_size("tensor")
    head = head_weight.reshape(blocks_dev * block_size, width_half)

    labels_n = lax.axis_size("label")
    slots = blocks.shape[1]
    targets = jnp.concatenate([blocks, offsets], axis=1).T
    targets = jnp.pad(targets, ((0, -targets.shape[0] % 8), (0, 0)))

    product = jnp.dot(hidden, enc_weight, preferred_element_type=F32).astype(BF16)
    pooled = scatter_label(product.reshape(labels_n, rows_here, width_half), 0)
    squares = lax.psum(jnp.sum(pooled * pooled, axis=1), "tensor")
    inverse = lax.rsqrt(squares / full_width + EPSILON)
    embedded = (pooled * inverse[:, None] * enc_gain[None, :]).astype(BF16)
    rows, targets, scores = gather_score(embedded, targets, head, 1)
    scores = scores.reshape(labels_n * rows_here, -1)
    rows = rows.reshape(labels_n * rows_here, width_half)
    targets = jnp.swapaxes(targets, 1, 2).reshape(labels_n * rows_here, -1)
    all_blocks, all_offsets = targets[:, :slots], targets[:, slots : slots + pos_count]

    label_ids = jnp.arange(block_size, dtype=jnp.int32)[None, :]
    first = lax.axis_index("label") * blocks_dev
    pieces = []
    for n in range(blocks_dev):
        named = all_blocks == first + n
        present = jnp.any(named, axis=1)[:, None]
        positive = jnp.zeros((), bool)
        for k in range(pos_count):
            positive = positive | (
                named[:, k : k + 1] & (all_offsets[:, k : k + 1] == label_ids)
            )
        here = scores[:, n * block_size : (n + 1) * block_size]
        weight_pos = (1.0 / propensity[n])[None, :]
        above = jnp.maximum(1.0 - here, 0.0)
        below = jnp.maximum(1.0 + here, 0.0)
        slope = jnp.where(
            positive, -2.0 * weight_pos * above + 2.0 * (1.0 - weight_pos) * below, 2.0 * below
        )
        pieces.append(jnp.where(present, slope / rows_here, 0.0).astype(BF16))
    slopes = jnp.concatenate(pieces, axis=1)

    back = jnp.dot(slopes, head, preferred_element_type=F32).astype(BF16)
    back = back.reshape(labels_n, rows_here, width_half)
    embed_grad, head_grad = scatter_label(back, 2, slopes, rows, blocks_dev)

    scaled = embed_grad * enc_gain[None, :]
    row_dot = lax.psum(jnp.sum(scaled * pooled, axis=1), "tensor")
    pooled_grad = (
        inverse[:, None] * (scaled - pooled * (inverse * inverse * row_dot / full_width)[:, None])
    ).astype(BF16)
    enc_grad = weight_grad(hidden, pooled_grad, 3)
    return (enc_grad, head_grad)


def solution(mesh):
    in_specs = (
        P("dp", "label"),
        P("label", "tensor"),
        P("tensor"),
        P("label", None, "tensor"),
        P("label", None),
        P(("dp", "label"), None),
        P(("dp", "label"), None),
    )
    out_specs = (P("label", "tensor"), P("label", "dp", "tensor"))
    return jax.shard_map(shards, mesh=mesh, in_specs=in_specs, out_specs=out_specs, check_vma=False)
```
